32 devices in a mesh: dp: 4 (over x, core), cell: 8 (over z, y).
Axes of the slice: x: 2, y: 2, z: 4, core: 2. Of those that a mesh axis runs over, the one named last changes fastest.
Arguments:
- probes: float32 [8, 32, 32, 128], P('cell', None, None, 'dp'), may hold values from -6 to 6
- diag_coef: float32 [8, 32, 32], P('cell'), may hold values from 1.5 to 3
- coupling: float32 [8, 32, 32], P('cell'), may hold values from 0.1 to 0.4
- jacobian: bfloat16 [16384, 8192], P('dp', 'cell'), may hold values from -0.0625 to 0.0625
- group_ids: int32 [16384], P('dp'), may hold values from 0 to 7
- group_weights: float32 [8], replicated, may hold values from 0.25 to 4
Outputs:
- action: float32 [8, 32, 32, 128], P('cell', None, None, 'dp')
The draws below stay inside these ranges and needn't reach their ends.
All inputs are finite; a program needn't handle non-finite values.
Results may differ from the reference program's by a relative error of at most 0.0036.
Values may be sent and summed in bfloat16 or wider, within the bound.
A program may use at most 64 MiB of HBM per device.

```python
import math
import jax
import jax.numpy as jnp
from jax import lax

CY = 32
CZ = 32
P_SIZE = 128
GROUPS = 8
NX = 8
CELLS = 8192
DATA = 16384


def plant(entries, key, low, largest):
    index_at = [jax.random.randint(jax.random.fold_in(key, axis), (), 0, length) for axis, length in enumerate(entries.shape)]
    widest = entries.shape.index(max(entries.shape))
    next_to = index_at[:widest] + [(index_at[widest] + 1) % entries.shape[widest]] + index_at[widest + 1:]
    return entries.at[tuple(index_at)].set(low).at[tuple(next_to)].set(largest)


def level_of(key, shape, cuts, smallest, top_value):
    factor_of = 1.0
    for position, shards_of in cuts:
        steps = jax.random.uniform(jax.random.fold_in(jax.random.fold_in(key, 6), position), (shards_of,), jnp.float32, smallest / len(cuts), top_value / len(cuts))
        factor_of = factor_of * jnp.repeat(jnp.exp(steps), shape[position] // shards_of).reshape((-1,) + (1,) * (len(shape) - 1 - position))
    return factor_of


def bell_draw(key, extent, spread, reach, shards=(), held_as=jnp.bfloat16):
    result = spread * jax.random.normal(key, extent, jnp.float32)
    if shards:
        result = result * level_of(key, extent, shards, -0.22, 0.18)
    return jnp.clip(result, -reach, reach).astype(held_as)


def setup_inputs(seed: int = 0) -> dict:
    keys = jax.random.split(jax.random.key(seed), 7)
    return {
        "probes": bell_draw(keys[0], (NX, CY, CZ, P_SIZE), 1.0, 6.0, ((0, 8), (3, 4)), jnp.float32),
        "diag_coef": jnp.clip(1.5 + 1.5 * jax.random.uniform(keys[1], (NX, CY, CZ), jnp.float32) ** level_of(keys[1], (NX, CY, CZ), ((0, 8),), -0.2, 0.2), 1.5, 3.0),
        "coupling": jnp.clip(jnp.exp(math.log(0.4) - 1.3862944 * jax.random.uniform(keys[2], (NX, CY, CZ), jnp.float32) ** level_of(keys[2], (NX, CY, CZ), ((0, 8),), -0.2, 0.2)), 0.1, 0.4),
        "jacobian": bell_draw(keys[3], (DATA, CELLS), CELLS ** -0.5, 0.0625, ((0, 4), (1, 8))),
        "group_ids": plant(jax.random.randint(keys[4], (DATA,), 0, GROUPS), jax.random.fold_in(keys[4], 1), 0, GROUPS - 1).astype(jnp.int32),
        "group_weights": jnp.clip(jnp.exp(jax.random.uniform(keys[5], (GROUPS,), jnp.float32, math.log(0.25), math.log(4.0))), 0.25, 4.0),
    }


def neighbour_sum(field):
    padded = jnp.pad(field, ((1, 1), (1, 1), (1, 1), (0, 0)))
    total = padded[2:, 1:-1, 1:-1] + padded[:-2, 1:-1, 1:-1]
    total = total + padded[1:-1, 2:, 1:-1] + padded[1:-1, :-2, 1:-1]
    return total + padded[1:-1, 1:-1, 2:] + padded[1:-1, 1:-1, :-2]


def reference(probes, diag_coef, coupling, jacobian, group_ids, group_weights):
    diag_full = diag_coef[..., None]
    coup_full = coupling[..., None]
    prior = diag_full * probes - neighbour_sum(coup_full * probes)
    prior = prior.astype(jnp.bfloat16).reshape(-1, probes.shape[3])
    predicted = jnp.dot(jacobian, prior, preferred_element_type=jnp.float32)
    datum_weight = group_weights[group_ids]
    weighted = (datum_weight[:, None] * predicted).astype(jnp.bfloat16)
    back = lax.dot_general(jacobian, weighted, (((0,), (0,)), ((), ())), preferred_element_type=jnp.float32)
    back = back.reshape(probes.shape)
    return probes + diag_full * back - coup_full * neighbour_sum(back)
```

```python
import functools

import jax
import jax.numpy as jnp
from jax import lax
from jax.experimental import pallas as pl
from jax.experimental.pallas import tpu as pltpu
from jax.sharding import PartitionSpec as P

PIECE = 128
NEAR = 2


def neighbours(field, width):
    cells = field.shape[1]
    lane = lax.broadcasted_iota(jnp.int32, (1, cells), 1)
    column = lane % width
    total = jnp.where(lane >= width, pltpu.roll(field, width, 1), 0.0)
    total += jnp.where(lane < cells - width, pltpu.roll(field, cells - width, 1), 0.0)
    total += jnp.where(column > 0, pltpu.roll(field, 1, 1), 0.0)
    return total + jnp.where(column < width - 1, pltpu.roll(field, cells - 1, 1), 0.0)


def kernel(
    nd, nc, width,
    probes_ref, coef_ref, ids_ref, gw_ref, jac_ref, out_ref,
    jac, halo_out, halo_in, fields, prior, near_out, near_in, keep, far_out, far_in,
    wrow, weighted, acc, back_out, back_in,
    jac_sem, halo_s, halo_r, gat_s, gat_r, near_s, near_r, far_s, far_r, wf_s, wf_r, wn_s, wn_r, dps_s, dps_r, halo2_s, halo2_r,
):
    dp = lax.axis_index("dp")
    cell = lax.axis_index("cell")
    near, far = lax.rem(cell, NEAR), lax.div(cell, NEAR)
    nf = nc // NEAR
    share, cells = probes_ref.shape
    rows = jac.shape[0]
    probes_all = fields.shape[0]
    groups = rows // (PIECE * nc)
    grows = rows // groups
    half = grows // NEAR
    partner = far * NEAR + (1 - near)

    def far_peer(d):
        return lax.rem(far + d, nf) * NEAR + near

    def dp_peer(d):
        return lax.rem(dp + d, nd)

    def jac_copy(g):
        block = pl.ds(g * grows, grows)
        return pltpu.make_async_copy(jac_ref.at[block], jac.at[block], jac_sem.at[g])

    def send(src, dst, ssem, rsem, **device):
        return pltpu.make_async_remote_copy(
            src_ref=src, dst_ref=dst, send_sem=ssem, recv_sem=rsem,
            device_id=device, device_id_type=pl.DeviceIdType.MESH,
        )

    for g in range(groups):
        jac_copy(g).start()

    other = jnp.where(near == 0, cell - 1, cell + 1)
    has_other = jnp.logical_and(other >= 0, other < nc)
    barrier = pltpu.get_barrier_semaphore()

    def greet(**device):
        pl.semaphore_signal(barrier, inc=1, device_id=device, device_id_type=pl.DeviceIdType.MESH)

    greet(cell=partner)

    @pl.when(has_other)
    def _():
        greet(cell=other)

    for d in range(1, nf):
        greet(cell=far_peer(d))
    for d in range(1, nd):
        greet(dp=dp_peer(d))

    coup = coef_ref[1:2, :]
    scaled = coup * probes_ref[...]
    halo_out[0] = scaled.astype(halo_out.dtype)
    pl.semaphore_wait(barrier, 1 + (nf - 1) + (nd - 1) + has_other.astype(jnp.int32))

    def halo(step, up, ssem, rsem):
        slot = 0 if up else 1
        return send(
            halo_out.at[step], halo_in.at[step, slot], ssem.at[slot], rsem.at[slot],
            cell=cell + 1 if up else cell - 1,
        )

    def halo_start(step, ssem, rsem):
        @pl.when(cell < nc - 1)
        def _():
            halo(step, True, ssem, rsem).start()

        @pl.when(cell > 0)
        def _():
            halo(step, False, ssem, rsem).start()

    def halo_sum(step, ssem, rsem):
        @pl.when(cell > 0)
        def _():
            halo(step, True, ssem, rsem).wait_recv()

        @pl.when(cell == 0)
        def _():
            halo_in[step, 0] = jnp.zeros((share, cells), halo_in.dtype)

        @pl.when(cell < nc - 1)
        def _():
            halo(step, False, ssem, rsem).wait_recv()

        @pl.when(cell == nc - 1)
        def _():
            halo_in[step, 1] = jnp.zeros((share, cells), halo_in.dtype)

        return halo_in[step, 0].astype(jnp.float32) + halo_in[step, 1].astype(jnp.float32)

    def halo_end(step, ssem, rsem):
        @pl.when(cell < nc - 1)
        def _():
            halo(step, True, ssem, rsem).wait_send()

        @pl.when(cell > 0)
        def _():
            halo(step, False, ssem, rsem).wait_send()

    halo_start(0, halo_s, halo_r)
    within = neighbours(scaled, width)
    ids = ids_ref[...]
    chosen = jnp.zeros(ids.shape, jnp.float32)
    for j in range(gw_ref.shape[0]):
        chosen = jnp.where(ids == j, gw_ref[j], chosen)
    wrow[...] = chosen

    own = pl.ds(pl.multiple_of(dp * share, share), share)
    total = within + halo_sum(0, halo_s, halo_r)
    fields[own, :] = (coef_ref[0:1, :] * probes_ref[...] - total).astype(fields.dtype)

    def gather(d):
        return send(fields.at[own], fields.at[own], gat_s.at[d], gat_r.at[d], dp=dp_peer(d))

    for d in range(1, nd):
        gather(d).start()
    for d in range(1, nd):
        gather(d).wait_recv()
    prior[...] = fields[...].astype(jnp.float32).T.astype(prior.dtype)

    def near_copy(g):
        return send(near_out.at[g], near_in.at[g], near_s.at[g], near_r.at[g], cell=partner)

    def far_copy(g, d):
        piece = pl.ds(pl.multiple_of(lax.rem(far + d, nf) * PIECE, PIECE), PIECE)
        return send(
            far_out.at[g, piece], far_in.at[g, d], far_s.at[g, d], far_r.at[g, d], cell=far_peer(d)
        )

    def wf_copy(g, d):
        k = (g * NEAR + near) * nf + far
        return send(weighted.at[k], weighted.at[k], wf_s.at[g, d], wf_r.at[g, d], cell=far_peer(d))

    def wn_copy(g):
        block = pl.ds((g * NEAR + near) * nf, nf)
        return send(weighted.at[block], weighted.at[block], wn_s.at[g], wn_r.at[g], cell=partner)

    def product(start, count):
        return jnp.dot(
            jac[pl.ds(pl.multiple_of(start, count), count), :], prior[...],
            preferred_element_type=jnp.float32,
        )

    def step_near(g):
        jac_copy(g).wait()
        near_out[g] = product(g * grows + (1 - near) * half, half).astype(near_out.dtype)
        near_copy(g).start()
        keep[g] = product(g * grows + near * half, half)

    def step_far(g):
        near_copy(g).wait_recv()
        summed = keep[g] + near_in[g].astype(jnp.float32)
        keep[g] = summed
        far_out[g] = summed.astype(far_out.dtype)
        for d in range(1, nf):
            far_copy(g, d).start()

    def step_weigh(g):
        total = keep[g, pl.ds(pl.multiple_of(far * PIECE, PIECE), PIECE), :]
        for d in range(1, nf):
            far_copy(g, d).wait_recv()
            total = total + far_in[g, d].astype(jnp.float32)
        k = (g * NEAR + near) * nf + far
        weighted[k] = (total.T * wrow[pl.ds(k, 1), :]).astype(weighted.dtype)
        for d in range(1, nf):
            wf_copy(g, d).start()

    def step_back(g):
        for d in range(1, nf):
            wf_copy(g, d).wait_recv()
        wn_copy(g).start()

    def step_product(g):
        wn_copy(g).wait_recv()
        pieces = grows // PIECE
        lhs = jnp.concatenate([weighted[g * pieces + k] for k in range(pieces)], axis=1)
        part = jnp.dot(lhs, jac[g * grows:(g + 1) * grows, :], preferred_element_type=jnp.float32)
        acc[...] = part if g == 0 else acc[...] + part

    steps = (step_near, step_far, step_weigh, step_back, step_product)
    for tick in range(groups + len(steps) - 1):
        for lag, step in enumerate(steps):
            if 0 <= tick - lag < groups:
                step(tick - lag)

    def scatter(d):
        return send(back_out.at[d], back_in.at[d], dps_s.at[d], dps_r.at[d], dp=dp_peer(d))

    for d in range(1, nd):
        block = pl.ds(pl.multiple_of(dp_peer(d) * share, share), share)
        back_out[d] = acc[block, :].astype(back_out.dtype)
        scatter(d).start()
    mine = acc[own, :]
    for d in range(1, nd):
        scatter(d).wait_recv()
        mine = mine + back_in[d].astype(jnp.float32)
    halo_out[1] = mine.astype(halo_out.dtype)
    halo_start(1, halo2_s, halo2_r)
    within = neighbours(mine, width)
    start = probes_ref[...] + coef_ref[0:1, :] * mine
    out_ref[...] = start - coup * (within + halo_sum(1, halo2_s, halo2_r))

    halo_end(0, halo_s, halo_r)
    halo_end(1, halo2_s, halo2_r)
    for d in range(1, nd):
        gather(d).wait_send()
        scatter(d).wait_send()
    for g in range(groups):
        near_copy(g).wait_send()
        wn_copy(g).wait_send()
        for d in range(1, nf):
            far_copy(g, d).wait_send()
            wf_copy(g, d).wait_send()


def shards(nd, nc, probes, diag_coef, coupling, jacobian, group_ids, group_weights):
    depth, height, width, share = probes.shape
    cells = depth * height * width
    rows = jacobian.shape[0]
    nf = nc // NEAR
    groups = rows // (PIECE * nc)
    grows = rows // groups
    half = grows // NEAR
    everyone = share * nd
    assert depth == 1 and nc % NEAR == 0 and groups * PIECE * nc == rows

    flat = probes.reshape(cells, share).T
    coefs = jnp.concatenate([diag_coef.reshape(1, cells), coupling.reshape(1, cells)], axis=0)
    low, dma = jnp.bfloat16, pltpu.SemaphoreType.DMA
    vmem = pl.BlockSpec(memory_space=pltpu.VMEM)
    out = pl.pallas_call(
        functools.partial(kernel, nd, nc, width),
        out_shape=jax.ShapeDtypeStruct((share, cells), jnp.float32),
        in_specs=[
            vmem, vmem, vmem,
            pl.BlockSpec(memory_space=pltpu.SMEM),
            pl.BlockSpec(memory_space=pl.ANY),
        ],
        out_specs=vmem,
        scratch_shapes=[
            pltpu.VMEM((rows, cells), low),
            pltpu.VMEM((2, share, cells), low),
            pltpu.VMEM((2, 2, share, cells), low),
            pltpu.VMEM((everyone, cells), low),
            pltpu.VMEM((cells, everyone), low),
            pltpu.VMEM((groups, half, everyone), low),
            pltpu.VMEM((groups, half, everyone), low),
            pltpu.VMEM((groups, half, everyone), jnp.float32),
            pltpu.VMEM((groups, half, everyone), low),
            pltpu.VMEM((groups, nf, PIECE, everyone), low),
            pltpu.VMEM((rows // PIECE, PIECE), jnp.float32),
            pltpu.VMEM((rows // PIECE, everyone, PIECE), low),
            pltpu.VMEM((everyone, cells), jnp.float32),
            pltpu.VMEM((nd, share, cells), low),
            pltpu.VMEM((nd, share, cells), low),
            dma((groups,)),
            dma((2,)), dma((2,)),
            dma((nd,)), dma((nd,)),
            dma((groups,)), dma((groups,)),
            dma((groups, nf)), dma((groups, nf)),
            dma((groups, nf)), dma((groups, nf)),
            dma((groups,)), dma((groups,)),
            dma((nd,)), dma((nd,)),
            dma((2,)), dma((2,)),
        ],
        compiler_params=pltpu.CompilerParams(
            collective_id=0, has_side_effects=True, vmem_limit_bytes=56 * 1024 * 1024
        ),
        cost_estimate=pl.CostEstimate(
            flops=4 * rows * cells * everyone, bytes_accessed=2 * rows * cells, transcendentals=0
        ),
    )(flat, coefs, group_ids.reshape(rows // PIECE, PIECE), group_weights, jacobian)
    return out.T.reshape(depth, height, width, share)


def solution(mesh):
    return jax.shard_map(
        functools.partial(shards, mesh.shape["dp"], mesh.shape["cell"]),
        mesh=mesh,
        in_specs=(
            P("cell", None, None, "dp"),
            P("cell", None, None),
            P("cell", None, None),
            P("dp", "cell"),
            P("dp"),
            P(),
        ),
        out_specs=P("cell", None, None, "dp"),
        check_vma=False,
    )
```

```python
import functools

import jax
import jax.numpy as jnp
from jax import lax
from jax.experimental import pallas as pl
from jax.experimental.pallas import tpu as pltpu
from jax.sharding import PartitionSpec as P

PIECE = 128
PARTS = 2


def as_row(ref, cells):
    height, width = ref.shape
    lane = lax.broadcasted_iota(jnp.int32, (width, cells), 1)
    spread = (lane % width == lax.broadcasted_iota(jnp.int32, (width, cells), 0)).astype(jnp.float32)
    wide = jnp.dot(
        ref[...], spread, precision=lax.Precision.HIGHEST, preferred_element_type=jnp.float32
    )
    lane = lax.broadcasted_iota(jnp.int32, (height, cells), 1)
    mine = lane // width == lax.broadcasted_iota(jnp.int32, (height, cells), 0)
    return jnp.sum(jnp.where(mine, wide, 0.0), axis=0, keepdims=True)


def neighbours(field, width):
    cells = field.shape[1]
    lane = lax.broadcasted_iota(jnp.int32, (1, cells), 1)
    column = lane % width
    total = jnp.where(lane >= width, pltpu.roll(field, width, 1), 0.0)
    total += jnp.where(lane < cells - width, pltpu.roll(field, cells - width, 1), 0.0)
    total += jnp.where(column > 0, pltpu.roll(field, 1, 1), 0.0)
    return total + jnp.where(column < width - 1, pltpu.roll(field, cells - 1, 1), 0.0)


def kernel(
    nd, nc,
    probes_ref, diag_ref, coup_ref, ids_ref, gw_ref, jac_ref, out_ref,
    jac, flat, halo_out, halo_in, fields, prior, near_out, near_in, keep, far_out, far_in,
    wrow, weighted, acc, back_out, back_in, own_sum,
    jac_sem, halo_s, halo_r, gat_s, gat_r, sum_s, sum_r, put_s, put_r, dps_s, dps_r,
):
    dp = lax.axis_index("dp")
    cell = lax.axis_index("cell")
    cells, share = probes_ref.shape
    width = diag_ref.shape[1]
    rows = jac.shape[0]
    groups = rows // (PIECE * nc)
    grows = rows // groups
    half = grows // 2
    levels = nc.bit_length() - 1
    part = cells // PARTS

    def bit(b):
        return lax.rem(lax.div(cell, 1 << b), 2)

    def peer(b):
        return cell + (1 - 2 * bit(b)) * (1 << b)

    def order(g):
        return (1, 0, *range(2, levels)) if g == 1 else tuple(range(levels))

    def dp_peer(d):
        return lax.rem(dp + d, nd)

    def jac_copy(g):
        block = pl.ds(g * grows, grows)
        return pltpu.make_async_copy(jac_ref.at[block], jac.at[block], jac_sem.at[g])

    def send(src, dst, ssem, rsem, **device):
        return pltpu.make_async_remote_copy(
            src_ref=src, dst_ref=dst, send_sem=ssem, recv_sem=rsem,
            device_id=device, device_id_type=pl.DeviceIdType.MESH,
        )

    other = cell + 2 * bit(0) - 1
    has_other = jnp.logical_and(other >= 0, other < nc)
    barrier = pltpu.get_barrier_semaphore()

    def greet(**device):
        pl.semaphore_signal(barrier, inc=1, device_id=device, device_id_type=pl.DeviceIdType.MESH)

    @pl.when(has_other)
    def _():
        greet(cell=other)

    for b in range(levels):
        greet(cell=peer(b))
    for d in range(1, nd):
        greet(dp=dp_peer(d))
    for g in range(groups):
        jac_copy(g).start()

    coup = as_row(coup_ref, cells)
    flat[...] = probes_ref[...].T
    scaled = coup * flat[...]

    def columns(h):
        return pl.ds(h * part, part)

    for h in range(PARTS):
        halo_out[0, h] = scaled[:, h * part:(h + 1) * part].astype(halo_out.dtype)
    pl.semaphore_wait(barrier, levels + (nd - 1) + has_other.astype(jnp.int32))

    def halo(step, h, up):
        slot = 0 if up else 1
        return send(
            halo_out.at[step, h], halo_in.at[step, h, slot],
            halo_s.at[step, h, slot], halo_r.at[step, h, slot],
            cell=cell + 1 if up else cell - 1,
        )

    def halo_start(step, h):
        @pl.when(cell < nc - 1)
        def _():
            halo(step, h, True).start()

        @pl.when(cell > 0)
        def _():
            halo(step, h, False).start()

    def halo_sum(step, h):
        @pl.when(cell > 0)
        def _():
            halo(step, h, True).wait_recv()

        @pl.when(cell == 0)
        def _():
            halo_in[step, h, 0] = jnp.zeros((share, part), halo_in.dtype)

        @pl.when(cell < nc - 1)
        def _():
            halo(step, h, False).wait_recv()

        @pl.when(cell == nc - 1)
        def _():
            halo_in[step, h, 1] = jnp.zeros((share, part), halo_in.dtype)

        return halo_in[step, h, 0].astype(jnp.float32) + halo_in[step, h, 1].astype(jnp.float32)

    def halo_end(step, h):
        @pl.when(cell < nc - 1)
        def _():
            halo(step, h, True).wait_send()

        @pl.when(cell > 0)
        def _():
            halo(step, h, False).wait_send()

    for h in range(PARTS):
        halo_start(0, h)
    diag = as_row(diag_ref, cells)
    within = diag * flat[...] - neighbours(scaled, width)
    ids = ids_ref[...]
    chosen = jnp.zeros(ids.shape, jnp.float32)
    for j in range(gw_ref.shape[0]):
        chosen = jnp.where(ids == j, gw_ref[j], chosen)
    wrow[...] = chosen

    own = pl.ds(pl.multiple_of(dp * share, share), share)

    def gather(d, h):
        block = fields.at[h, own]
        return send(block, block, gat_s.at[d, h], gat_r.at[d, h], dp=dp_peer(d))

    for h in range(PARTS):
        total = within[:, h * part:(h + 1) * part] - halo_sum(0, h)
        fields[h, own] = total.astype(fields.dtype)
        for d in range(1, nd):
            gather(d, h).start()
    for h in range(PARTS):
        for d in range(1, nd):
            gather(d, h).wait_recv()
        prior[columns(h), :] = fields[h].astype(jnp.float32).T.astype(prior.dtype)

    def block(g, i):
        start = 0
        for level in range(1, i + 1):
            size = half >> level
            mine = bit(order(g)[level])
            kept, sent, start = start + mine * size, start + (1 - mine) * size, start + mine * size
        return kept, sent, size

    def ds(start, size):
        return pl.ds(pl.multiple_of(start, size), size)

    def sum_copy(g, i):
        ssem, rsem, to = sum_s.at[g, i], sum_r.at[g, i], peer(order(g)[i])
        if i == 0:
            return send(near_out.at[g], near_in.at[g], ssem, rsem, cell=to)
        kept, sent, size = block(g, i)
        return send(far_out.at[g, ds(sent, size)], far_in.at[g, ds(kept, size)], ssem, rsem, cell=to)

    def arrived(g, i, skip, size):
        if i == 0:
            return near_in[g, ds(skip, size), :].astype(jnp.float32)
        return far_in[g, ds(block(g, i)[1] + skip, size), :].astype(jnp.float32)

    def place(g):
        where = 0
        for b in order(g):
            where = where * 2 + bit(b)
        return where

    def put_copy(g, i):
        count = 1 << (levels - 1 - i)
        pieces = weighted.at[pl.ds(g * nc + lax.div(place(g), count) * count, count)]
        return send(pieces, pieces, put_s.at[g, i], put_r.at[g, i], cell=peer(order(g)[i]))

    def product(start, count):
        return jnp.dot(
            jac[pl.ds(pl.multiple_of(start, count), count), :], prior[...],
            preferred_element_type=jnp.float32,
        )

    def first(g):
        mine = bit(order(g)[0])
        jac_copy(g).wait()
        near_out[g] = product(g * grows + (1 - mine) * half, half).astype(near_out.dtype)
        sum_copy(g, 0).start()
        keep[g] = product(g * grows + mine * half, half)

    def add(g, i):
        sum_copy(g, i - 1).wait_recv()
        kept, sent, size = block(g, i)
        mine = bit(order(g)[i])
        leaves = keep[g, ds(sent, size), :] + arrived(g, i - 1, (1 - mine) * size, size)
        far_out[g, ds(sent, size), :] = leaves.astype(far_out.dtype)
        sum_copy(g, i).start()
        keep[g, ds(kept, size), :] += arrived(g, i - 1, mine * size, size)

    def weigh(g):
        sum_copy(g, levels - 1).wait_recv()
        kept, _, size = block(g, levels - 1)
        total = keep[g, ds(kept, size), :] + arrived(g, levels - 1, 0, size)
        k = g * nc + place(g)
        weighted[k] = (total.T * wrow[pl.ds(k, 1), :]).astype(weighted.dtype)
        put_copy(g, levels - 1).start()

    def hand(g, i):
        put_copy(g, i + 1).wait_recv()
        put_copy(g, i).start()

    def scatter(d, h):
        return send(
            back_out.at[d, h], back_in.at[d, h], dps_s.at[d, h], dps_r.at[d, h], dp=dp_peer(d)
        )

    def last(g):
        put_copy(g, 0).wait_recv()
        lhs = jnp.concatenate([weighted[g * nc + k] for k in range(nc)], axis=1)
        for h in range(PARTS):
            back = jnp.dot(
                lhs, jac[pl.ds(g * grows, grows), columns(h)], preferred_element_type=jnp.float32
            )
            acc[h] = back if g == 0 else acc[h] + back
            if g == groups - 1:
                for d in range(1, nd):
                    theirs = pl.ds(pl.multiple_of(dp_peer(d) * share, share), share)
                    back_out[d, h] = acc[h, theirs].astype(back_out.dtype)
                    scatter(d, h).start()

    steps = [first]
    steps += [functools.partial(add, i=i) for i in range(1, levels)]
    steps += [weigh]
    steps += [functools.partial(hand, i=i) for i in reversed(range(levels - 1))]
    steps += [last]
    for tick in range(groups + len(steps) - 1):
        for lag, step in enumerate(steps):
            if 0 <= tick - lag < groups:
                step(tick - lag)

    for h in range(PARTS):
        mine = acc[h, own]
        for d in range(1, nd):
            scatter(d, h).wait_recv()
            mine = mine + back_in[d, h].astype(jnp.float32)
        own_sum[:, columns(h)] = mine
        halo_out[1, h] = mine.astype(halo_out.dtype)
        halo_start(1, h)
    mine = own_sum[...]
    within = neighbours(mine, width)
    start = flat[...] + diag * mine - coup * within
    for h in range(PARTS):
        cut = slice(h * part, (h + 1) * part)
        out_ref[columns(h), :] = (start[:, cut] - coup[:, cut] * halo_sum(1, h)).T

    for h in range(PARTS):
        halo_end(0, h)
        halo_end(1, h)
        for d in range(1, nd):
            gather(d, h).wait_send()
            scatter(d, h).wait_send()
    for g in range(groups):
        for i in range(levels):
            sum_copy(g, i).wait_send()
            put_copy(g, i).wait_send()


def shards(nd, nc, probes, diag_coef, coupling, jacobian, group_ids, group_weights):
    depth, height, width, share = probes.shape
    cells = depth * height * width
    rows = jacobian.shape[0]
    levels = nc.bit_length() - 1
    groups = rows // (PIECE * nc)
    half = rows // groups // 2
    everyone = share * nd
    part = cells // PARTS
    assert depth == 1 and nc == 1 << levels and levels >= 2 and groups * PIECE * nc == rows

    low, dma = jnp.bfloat16, pltpu.SemaphoreType.DMA
    vmem = pl.BlockSpec(memory_space=pltpu.VMEM)
    out = pl.pallas_call(
        functools.partial(kernel, nd, nc),
        out_shape=jax.ShapeDtypeStruct((cells, share), jnp.float32),
        in_specs=[
            vmem, vmem, vmem, vmem,
            pl.BlockSpec(memory_space=pltpu.SMEM),
            pl.BlockSpec(memory_space=pl.ANY),
        ],
        out_specs=vmem,
        scratch_shapes=[
            pltpu.VMEM((rows, cells), low),
            pltpu.VMEM((share, cells), jnp.float32),
            pltpu.VMEM((2, PARTS, share, part), low),
            pltpu.VMEM((2, PARTS, 2, share, part), low),
            pltpu.VMEM((PARTS, everyone, part), low),
            pltpu.VMEM((cells, everyone), low),
            pltpu.VMEM((groups, half, everyone), low),
            pltpu.VMEM((groups, half, everyone), low),
            pltpu.VMEM((groups, half, everyone), jnp.float32),
            pltpu.VMEM((groups, half, everyone), low),
            pltpu.VMEM((groups, half, everyone), low),
            pltpu.VMEM((rows // PIECE, PIECE), jnp.float32),
            pltpu.VMEM((rows // PIECE, everyone, PIECE), low),
            pltpu.VMEM((PARTS, everyone, part), jnp.float32),
            pltpu.VMEM((nd, PARTS, share, part), low),
            pltpu.VMEM((nd, PARTS, share, part), low),
            pltpu.VMEM((share, cells), jnp.float32),
            dma((groups,)),
            dma((2, PARTS, 2)), dma((2, PARTS, 2)),
            dma((nd, PARTS)), dma((nd, PARTS)),
            dma((groups, levels)), dma((groups, levels)),
            dma((groups, levels)), dma((groups, levels)),
            dma((nd, PARTS)), dma((nd, PARTS)),
        ],
        compiler_params=pltpu.CompilerParams(
            collective_id=0, has_side_effects=True, vmem_limit_bytes=56 * 1024 * 1024
        ),
        cost_estimate=pl.CostEstimate(
            flops=4 * rows * cells * everyone, bytes_accessed=2 * rows * cells, transcendentals=0
        ),
    )(
        probes.reshape(cells, share),
        diag_coef.reshape(height, width),
        coupling.reshape(height, width),
        group_ids.reshape(rows // PIECE, PIECE),
        group_weights,
        jacobian,
    )
    return out.reshape(depth, height, width, share)


def solution(mesh):
    return jax.shard_map(
        functools.partial(shards, mesh.shape["dp"], mesh.shape["cell"]),
        mesh=mesh,
        in_specs=(
            P("cell", None, None, "dp"),
            P("cell", None, None),
            P("cell", None, None),
            P("dp", "cell"),
            P("dp"),
            P(),
        ),
        out_specs=P("cell", None, None, "dp"),
        check_vma=False,
    )
```
